256 devices in a mesh: dp: 64 (over z, x, core), tower: 2 (over y_hi), replica: 2 (over y_lo).
Axes of the slice: x: 4, y: 4 (y_hi: 2, y_lo: 2; y = y_hi * 2 + y_lo), z: 8, core: 2. Of those that a mesh axis runs over, the one named last changes fastest.
Arguments:
- feature_vectors: bfloat16 [2, 163840, 1152], P('tower', ('replica', 'dp')), parts along dimension 1, may hold values from -6 to 6
- sample_source_label: int32 [163840], P('replica'), parts along dimension 0, may hold values from 0 to 40959
- sharpness_factor_array: float32 [1], replicated, may hold values from 20 to 40
- logit_offset_array: float32 [1], replicated, may hold values from -3 to 0
Outputs:
- grad_embeddings: float32 [2, 163840, 1152], P('tower', ('replica', 'dp')), parts along dimension 1
The draws below stay inside these ranges and needn't reach their ends.
There are 2 independent parts, one for each index of `replica`. The reference program is written for one: setup_inputs(seed, part) draws one part's arguments, and reference() takes and returns one part's arrays. A program takes and returns all parts, laid end to end along the dimension named above; an argument that names none is the same for every part. Nothing has to cross between parts.
All inputs are finite; a program needn't handle non-finite values.
Results may differ from the reference program's by a relative error of at most 0.0058.
Values may be sent and summed in bfloat16 or wider, within the bound.
No kernel may reach another device: no remote copies, remote signals or barrier semaphores. Data moves between devices by JAX's collectives and lax.ppermute only.
A program may use at most 128 MiB of HBM per device.

```python
import jax
import jax.numpy as jnp
from jax import lax

D = 1152
ROWS = 640
STEPS = 4
PAIRS = 81920
N_DP = 64


def touch_ends(drawn, key, low, top_value):
    place = [jax.random.randint(jax.random.fold_in(key, axis), (), 0, length) for axis, length in enumerate(drawn.shape)]
    main_axis = drawn.shape.index(max(drawn.shape))
    neighbour = place[:main_axis] + [(place[main_axis] + 1) % drawn.shape[main_axis]] + place[main_axis + 1:]
    return drawn.at[tuple(place)].set(low).at[tuple(neighbour)].set(top_value)


def block_levels(own_key, dims, shards, least, high):
    loudness, own = 1.0, jax.random.fold_in(own_key, 6)
    for axis_at, blocks in shards:
        steps = jnp.exp(jax.random.uniform(jax.random.fold_in(own, axis_at), (blocks,), jnp.float32, least / len(shards), high / len(shards)))
        loudness = loudness * jnp.repeat(steps, dims[axis_at] // blocks).reshape([-1 if axis == axis_at else 1 for axis in range(len(dims))])
    return loudness


def gaussian(rng, shape, width, most, cuts=(), dtype=jnp.bfloat16):
    values = jax.random.normal(rng, shape, jnp.float32) * width
    if len(cuts) > 0:
        values = block_levels(rng, shape, cuts, -0.22, 0.18) * values
    return jnp.clip(values, min=-most, max=most).astype(dtype)


def setup_inputs(seed: int = 0, part: int = 0) -> dict:
    key_of = jax.random.split(jax.random.key(seed), 5)
    part_keys = jax.random.split(jax.random.fold_in(key_of[4], part), 5)
    feature_vectors = gaussian(part_keys[0], (2, PAIRS, D), 1.0, 6.0, ((0, 2), (1, 64)))
    sample_source_label = touch_ends(jax.random.randint(part_keys[1], (PAIRS,), 0, ROWS * N_DP), jax.random.fold_in(part_keys[1], 1), 0, (ROWS * N_DP) - 1).astype(jnp.int32)
    sharpness_factor_array = jnp.clip(jax.random.uniform(key_of[2], (1,), jnp.float32, 20.0, 40.0), 20.0, 40.0)
    logit_offset_array = jnp.clip(jax.random.uniform(key_of[3], (1,), jnp.float32, -3.0, 0.0), -3.0, 0.0)
    return dict(feature_vectors=feature_vectors, sample_source_label=sample_source_label, sharpness_factor_array=sharpness_factor_array, logit_offset_array=logit_offset_array)


epsilon = 1e-06

def unit_rows(block):
    widened = block.astype(jnp.float32)
    inverse_norm = lax.rsqrt(lax.optimization_barrier(jnp.sum(widened * widened, axis=-1, keepdims=True)) + epsilon)
    return (widened * inverse_norm, inverse_norm)

def match_factors(picture_vectors, caption_vectors, picture_labels, caption_labels, sharpness_multiplier, shift_amount_scalar):
    similarity_matrix = lax.dot_general(picture_vectors, caption_vectors, (((1,), (1,)), ((), ())), preferred_element_type=jnp.float32)
    affinity_scores = similarity_matrix * sharpness_multiplier + shift_amount_scalar
    match_polarity = jnp.where(picture_labels[:, None] == caption_labels[None, :], 1.0, -1.0).astype(jnp.float32)
    return (-(match_polarity * sharpness_multiplier) * jax.nn.sigmoid(-match_polarity * affinity_scores)).astype(jnp.bfloat16)

def reference(feature_vectors, sample_source_label, sharpness_factor_array, logit_offset_array):
    block_groups = 2 * N_DP
    sharpness_multiplier = sharpness_factor_array[0]
    shift_amount_scalar = logit_offset_array[0]
    unit_all, inverse_norm = unit_rows(feature_vectors)
    normed = unit_all.astype(jnp.bfloat16)
    image_blocks = normed[0].reshape(block_groups, ROWS, D)
    text_blocks = normed[1].reshape(block_groups, ROWS, D)
    id_blocks = sample_source_label.reshape(block_groups, ROWS)
    image_grad = jnp.zeros((block_groups, ROWS, D), jnp.float32)
    text_grad = jnp.zeros((block_groups, ROWS, D), jnp.float32)
    for offset in range(STEPS):
        moved_texts = jnp.roll(text_blocks, offset, axis=0)
        moved_ids = jnp.roll(id_blocks, offset, axis=0)

        def one_block(input_operands):
            picture_vectors, caption_vectors, picture_labels, caption_labels = input_operands
            coefficient_matrix = match_factors(picture_vectors, caption_vectors, picture_labels, caption_labels, sharpness_multiplier, shift_amount_scalar)
            image_part = jnp.dot(coefficient_matrix, caption_vectors, preferred_element_type=jnp.float32)
            text_part = lax.dot_general(coefficient_matrix, picture_vectors, (((0,), (0,)), ((), ())), preferred_element_type=jnp.float32)
            return (image_part, text_part)
        image_part, text_part = lax.map(one_block, (image_blocks, moved_texts, id_blocks, moved_ids))
        image_grad = image_grad + image_part
        text_grad = text_grad + jnp.roll(text_part, -offset, axis=0)
    grads = jnp.stack([image_grad.reshape(-1, D), text_grad.reshape(-1, D)])
    projected_embedding = lax.optimization_barrier(jnp.sum(unit_all * grads, axis=-1, keepdims=True))
    return inverse_norm * (grads - unit_all * projected_embedding)
```

```python
import jax
import jax.numpy as jnp
from jax import lax
from jax.sharding import PartitionSpec as P

ROWS = 640
N_BLOCKS = 128
epsilon = 1e-06

FIRST = ((0, 256), (256, 384))
SECOND = ((0, 256), (256, 256), (512, 128))


def swapped(array):
    return lax.ppermute(array, "tower", [(0, 1), (1, 0)])


def passed_on(array):
    length = lax.axis_size("dp")
    pairs = []
    for i in range(length):
        pairs.append((2 * i, 2 * ((i + 1) % length)))
        pairs.append((2 * i + 1, 2 * ((i - 1) % length) + 1))
    return lax.ppermute(array, ("dp", "tower"), pairs)


def weights(own, other, own_labels, other_labels, sharpness, shift):
    inner = lax.dot_general(
        own, other, (((1,), (1,)), ((), ())), preferred_element_type=jnp.float32
    )
    logit = inner * sharpness + shift
    same = own_labels[:, None] == other_labels[None, :]
    polarity = jnp.where(same, 1.0, -1.0).astype(jnp.float32)
    return (-(polarity * sharpness) * jax.nn.sigmoid(-polarity * logit)).astype(jnp.bfloat16)


def per_device(feature_vectors, sample_source_label, sharpness_factor_array, logit_offset_array):
    sharpness = sharpness_factor_array[0]
    shift = logit_offset_array[0]
    tower = lax.axis_index("tower")
    dp = lax.axis_index("dp")
    blocks = feature_vectors.reshape(2, ROWS, -1)
    own = jnp.where(tower == 0, blocks, blocks[::-1])
    widened = own.astype(jnp.float32)
    inverse_norm = lax.rsqrt(jnp.sum(widened * widened, axis=-1, keepdims=True) + epsilon)
    unit = widened * inverse_norm
    normed = unit.astype(jnp.bfloat16)

    label_blocks = sample_source_label.reshape(N_BLOCKS, ROWS)

    def labels_at(block):
        return lax.dynamic_index_in_dim(label_blocks, block % N_BLOCKS, 0, keepdims=False)

    own_labels = [labels_at(2 * dp + tower), labels_at(2 * dp + 1 - tower)]
    other_labels = [
        labels_at(jnp.where(tower == 0, 2 * dp + 1 - j, 2 * dp + j)) for j in range(5)
    ]
    grads = [jnp.zeros((ROWS, own.shape[-1]), jnp.float32) for _ in range(2)]

    def update(j, start, size, chunk):
        labels = other_labels[j][start : start + size]
        for i in range(2):
            if 0 <= j - (1 - i) <= 3:
                w = weights(normed[i], chunk, own_labels[i], labels, sharpness, shift)
                grads[i] = grads[i] + jnp.dot(w, chunk, preferred_element_type=jnp.float32)

    first = [swapped(normed[0, a : a + n]) for a, n in FIRST]
    second = [swapped(normed[1, a : a + n]) for a, n in SECOND]
    first_next = [passed_on(c) for c in first]
    first_last = [passed_on(c) for c in first_next]
    second_next = [passed_on(c) for c in second]
    for (a, n), c in zip(FIRST, first):
        update(0, a, n, c)
    for (a, n), c in zip(FIRST, first_next):
        update(2, a, n, c)
    for (a, n), c in zip(FIRST, first_last):
        update(4, a, n, c)
    for (a, n), c, c_next in zip(SECOND, second, second_next):
        update(1, a, n, c)
        update(3, a, n, c_next)
    g = jnp.stack(grads)
    projected = jnp.sum(unit * g, axis=-1, keepdims=True)
    out = inverse_norm * (g - unit * projected)
    out = jnp.where(tower == 0, out, out[::-1])
    return out.reshape(1, 2 * ROWS, -1)


def solution(mesh):
    placed = (P("tower", ("replica", "dp"), None), P("replica"), P(), P())
    return jax.shard_map(
        per_device,
        mesh=mesh,
        in_specs=placed,
        out_specs=P("tower", ("replica", "dp"), None),
        check_vma=False,
    )
```

```python
import functools

import jax
import jax.numpy as jnp
from jax import lax
from jax.experimental import pallas as pl
from jax.experimental.pallas import tpu as pltpu
from jax.sharding import PartitionSpec as P

ROWS = 640
N_BLOCKS = 128
LANES = 128
TILE = 320
PER_BLOCK = ROWS // TILE
VMEM_LIMIT = 28 * 2**20
epsilon = 1e-06

FIRST = ((0, 256), (256, 384))
SECOND = ((0, 384), (384, 256))

VMEM = pl.BlockSpec(memory_space=pltpu.VMEM)
SMEM = pl.BlockSpec(memory_space=pltpu.SMEM)
ANY = pl.BlockSpec(memory_space=pl.ANY)

Y1, X, A, Y2, Z, B = range(6)


def moved(array, step, cores=None):
    length = lax.axis_size("dp")
    pairs = []
    for i in range(length):
        for tower, sign in ((0, 1), (1, -1)):
            if cores is None or (i % 2) ^ tower == cores:
                pairs.append((2 * i + tower, 2 * ((i + sign * step) % length) + tower))
    return lax.ppermute(array, ("dp", "tower"), pairs)


def swapped(name, array):
    with jax.named_scope(name):
        return lax.ppermute(array, "tower", [(0, 1), (1, 0)])


def onward(name, array):
    with jax.named_scope(name):
        return moved(array, 1)


def back(name, array):
    with jax.named_scope(name):
        return moved(array, -1)


def chip_onward(name, array):
    with jax.named_scope(name):
        return moved(array, 2, 0)


def core_onward(name, array):
    with jax.named_scope(name):
        return moved(array, 1, 0)


def after(array, token):
    return lax.optimization_barrier((array, token))[0]


def inverse_norm_of(rows):
    return lax.rsqrt(jnp.sum(rows * rows, axis=-1, keepdims=True) + epsilon)


def lead_kernel(place_ref, features_ref, out_ref, raw_ref, sem):
    count = out_ref.shape[0]
    start = pl.multiple_of((1 - place_ref[1]) * ROWS, ROWS)
    copy = pltpu.make_async_copy(features_ref.at[0, pl.ds(start, count), :], raw_ref, sem)
    copy.start()
    copy.wait()
    rows = raw_ref[...].astype(jnp.float32)
    out_ref[...] = (rows * inverse_norm_of(rows)).astype(jnp.bfloat16)


def lead_rows(place, features, count):
    width = features.shape[-1]
    return pl.pallas_call(
        lead_kernel,
        out_shape=jax.ShapeDtypeStruct((count, width), jnp.bfloat16),
        in_specs=[SMEM, ANY],
        out_specs=VMEM,
        scratch_shapes=[pltpu.VMEM((count, width), jnp.bfloat16), pltpu.SemaphoreType.DMA],
        compiler_params=pltpu.CompilerParams(vmem_limit_bytes=60 * 2**20),
    )(place, features)


def norm_kernel(parts, place_ref, lead_ref, features_ref, out_ref, *part_refs):
    tower, core = place_ref[0], place_ref[1]
    for tile in range(2 * PER_BLOCK):
        block, within = tile // PER_BLOCK, tile % PER_BLOCK
        start = pl.multiple_of((block ^ tower) * ROWS + within * TILE, TILE)
        rows = features_ref[0, pl.ds(start, TILE), :].astype(jnp.float32)
        out_ref[pl.ds(tile * TILE, TILE), :] = (rows * inverse_norm_of(rows)).astype(jnp.bfloat16)
    for (second, start, size), part_ref in zip(parts, part_refs):
        block = (core if second else 1 - core) ^ tower
        part_ref[...] = out_ref[pl.ds(pl.multiple_of(block * ROWS + start, LANES), size), :]


def norm_rows(place, lead, features, parts):
    width = features.shape[-1]
    sizes = [2 * ROWS] + [n for _, _, n in parts]
    return pl.pallas_call(
        functools.partial(norm_kernel, parts),
        out_shape=[jax.ShapeDtypeStruct((n, width), jnp.bfloat16) for n in sizes],
        in_specs=[SMEM, ANY, VMEM],
        out_specs=[VMEM] * len(sizes),
        compiler_params=pltpu.CompilerParams(vmem_limit_bytes=VMEM_LIMIT),
    )(place, lead, features)


def label_kernel(blocks_ref, labels_ref, own_ref, other_ref):
    per_block = ROWS // LANES
    for slot in range(8):
        for i in range(per_block):
            line = labels_ref[pl.ds(blocks_ref[slot] * per_block + i, 1), :]
            if slot < 6:
                other_ref[slot, :, pl.ds(i * LANES, LANES)] = line
            else:
                rows = pl.ds((slot - 6) * ROWS + i * LANES, LANES)
                own_ref[rows, :] = jnp.transpose(jnp.broadcast_to(line, (LANES, LANES)))


def label_rows(blocks, labels):
    return pl.pallas_call(
        label_kernel,
        out_shape=[
            jax.ShapeDtypeStruct((2 * ROWS, LANES), jnp.int32),
            jax.ShapeDtypeStruct((6, 1, ROWS), jnp.int32),
        ],
        in_specs=[SMEM, VMEM],
        out_specs=[VMEM, VMEM],
        compiler_params=pltpu.CompilerParams(vmem_limit_bytes=VMEM_LIMIT),
    )(blocks, labels.reshape(-1, LANES))


def update_kernel(pieces, spans, tile_rows, has_old, finish, place_ref, sharpness_ref, shift_ref, *refs):
    refs = list(refs)
    own_ref, own_label_ref, other_label_ref = refs[:3]
    del refs[:3]
    tower, role = place_ref[0], place_ref[2]
    sharpness, shift = sharpness_ref[0], shift_ref[0]
    chunk_refs = [[refs.pop(0) for _ in range(count)] for _, _, _, count in pieces]
    old_ref = refs.pop(0) if has_old else None
    if finish:
        features_ref, out_ref, others_ref, staging, sems = refs
    else:
        out_ref, others_ref = refs
    at, labels = 0, []
    for (slot, start, size, _), choices in zip(pieces, chunk_refs):
        rows = pl.ds(at, size)
        if len(choices) == 1:
            others_ref[rows, :] = choices[0][...]
        else:

            @pl.when(role == 0)
            def _():
                others_ref[rows, :] = choices[0][...]

            @pl.when(role != 0)
            def _():
                others_ref[rows, :] = choices[1][...]

        labels.append(other_label_ref[slot][:, start : start + size])
        at += size
    labels = jnp.concatenate(labels, axis=1)
    copies = []
    for tile in range(2 * ROWS // tile_rows):
        block, within = tile * tile_rows // ROWS, tile * tile_rows % ROWS
        low, high = spans[block]
        rows = pl.ds(tile * tile_rows, tile_rows)
        others = others_ref[pl.ds(low, high - low), :]
        inner = lax.dot_general(
            own_ref[rows, :], others, (((1,), (1,)), ((), ())), preferred_element_type=jnp.float32
        )
        logit = inner * sharpness + shift
        same = own_label_ref[rows, :1] == labels[:, low:high]
        grown = jnp.exp(jnp.where(same, logit, -logit))
        weight = (jnp.where(same, -sharpness, sharpness) / (1.0 + grown)).astype(jnp.bfloat16)
        total = jnp.dot(weight, others, preferred_element_type=jnp.float32)
        if has_old:
            total = old_ref[rows, :] + total
        if not finish:
            out_ref[rows, :] = total
            continue
        native = pl.ds(pl.multiple_of((block ^ tower) * ROWS + within, tile_rows), tile_rows)
        raw = features_ref[0, native, :].astype(jnp.float32)
        inverse_norm = inverse_norm_of(raw)
        unit = raw * inverse_norm
        projected = jnp.sum(unit * total, axis=-1, keepdims=True)
        staging[tile] = inverse_norm * (total - unit * projected)
        copy = pltpu.make_async_copy(staging.at[tile], out_ref.at[0, native, :], sems.at[tile])
        copy.start()
        copies.append(copy)
    for copy in copies:
        copy.wait()


def update(scalars, own, own_labels, other_labels, pieces, spans, grads, features=None):
    width = own.shape[-1]
    finish = features is not None
    chunks = [array for *_, arrays in pieces for array in arrays]
    pieces = [(slot, start, size, len(arrays)) for slot, start, size, arrays in pieces]
    operands = [*scalars, own, own_labels, other_labels, *chunks]
    aliases = {}
    if grads is not None:
        if not finish:
            aliases = {len(operands): 0}
        operands.append(grads)
    depth = sum(size for _, _, size, _ in pieces)
    scratch = [pltpu.VMEM((depth, width), jnp.bfloat16)]
    tile_rows = TILE if finish else ROWS
    if finish:
        operands.append(features)
        tiles = 2 * ROWS // tile_rows
        scratch += [pltpu.VMEM((tiles, tile_rows, width), jnp.float32), pltpu.SemaphoreType.DMA((tiles,))]
    shape = (1, 2 * ROWS, width) if finish else (2 * ROWS, width)
    return pl.pallas_call(
        functools.partial(update_kernel, pieces, spans, tile_rows, grads is not None, finish),
        out_shape=jax.ShapeDtypeStruct(shape, jnp.float32),
        in_specs=[SMEM] * len(scalars) + [VMEM] * (len(operands) - len(scalars)),
        out_specs=ANY if finish else VMEM,
        scratch_shapes=scratch,
        input_output_aliases=aliases,
        compiler_params=pltpu.CompilerParams(vmem_limit_bytes=VMEM_LIMIT),
        cost_estimate=pl.CostEstimate(flops=1, bytes_accessed=1, transcendentals=0),
    )(*operands)


def per_device(feature_vectors, sample_source_label, sharpness_factor_array, logit_offset_array):
    tower = lax.axis_index("tower")
    dp = lax.axis_index("dp")
    core = dp % 2
    role = core ^ tower
    place = jnp.stack([tower, core, role]).astype(jnp.int32)

    a0, a1 = (n for _, n in FIRST)
    b0, b1 = (n for _, n in SECOND)
    lead = lead_rows(place, feature_vectors, a0)
    parts = [(False, *FIRST[1]), (True, *SECOND[0]), (True, *SECOND[1])]
    normed, part, *early = norm_rows(place, lead, feature_vectors, parts)

    def block_at(index):
        chip = 4 * (dp // 2)
        return jnp.where(tower == 0, chip + index, chip + 3 - index) % N_BLOCKS

    held = [1 + role, 3 * role - 2, 5 * role - 3, role - 1, 3 * role, -role, 2 * role, 2 * role + 1]
    blocks = jnp.stack([block_at(index) for index in held]).astype(jnp.int32)
    own_labels, other_labels = label_rows(blocks, sample_source_label)
    scalars = (place, sharpness_factor_array, logit_offset_array)
    run = functools.partial(update, scalars, normed, own_labels, other_labels)

    y0 = swapped("y0", lead)
    y1 = swapped("y1", part)
    y0 = after(y0, normed)
    e0, e1 = back("e0", early[0]), back("e1", after(early[1], y0))
    y2, y3 = swapped("y2", e0), swapped("y3", e1)
    x0, w0 = onward("x0", y0), chip_onward("w0", y0)
    x1, w1 = onward("x1", y1), chip_onward("w1", y1)

    def stage(cut, y, x, w):
        return [(A, *cut, (w, y)), (X, *cut, (x,)), (Y1, *cut, (y,))]

    grads = run(stage(FIRST[0], y0, x0, w0), ((0, 2 * a0), (a0, 3 * a0)), None)
    y2 = after(y2, grads)
    z2, c2 = back("z2", y2), core_onward("c2", y2)
    grads = run(stage(FIRST[1], y1, x1, w1), ((0, 2 * a1), (a1, 3 * a1)), grads)
    y3 = after(y3, grads)
    z3, c3 = back("z3", y3), core_onward("c3", y3)
    grads = run(
        [(B, *SECOND[0], (z2, c2)), (Y2, *SECOND[0], (y2,)), (Y2, *SECOND[1], (y3,)), (Z, *SECOND[0], (z2,))],
        ((0, 2 * b0 + b1), (b0, 3 * b0 + b1)),
        grads,
    )
    return run(
        [(B, *SECOND[1], (z3, c3)), (Z, *SECOND[1], (z3,))],
        ((0, b1), (b1, 2 * b1)),
        grads,
        features=feature_vectors,
    )


def solution(mesh):
    placed = (P("tower", ("replica", "dp"), None), P("replica"), P(), P())
    return jax.shard_map(
        per_device,
        mesh=mesh,
        in_specs=placed,
        out_specs=P("tower", ("replica", "dp"), None),
        check_vma=False,
    )
```

```python
import functools

import jax
import jax.numpy as jnp
from jax import lax
from jax.experimental import pallas as pl
from jax.experimental.pallas import tpu as pltpu
from jax.sharding import PartitionSpec as P

ROWS = 640
N_BLOCKS = 128
LANES = 128
TILE = 320
PER_BLOCK = ROWS // TILE
VMEM_LIMIT = 16 * 2**20
epsilon = 1e-06

FIRST = ((0, 256), (256, 384))
SECOND = ((0, 384), (384, 256))

VMEM = pl.BlockSpec(memory_space=pltpu.VMEM)
SMEM = pl.BlockSpec(memory_space=pltpu.SMEM)
ANY = pl.BlockSpec(memory_space=pl.ANY)

Y1, X, A, Y2, Z, B = range(6)


def moved(array, step, cores=None):
    length = lax.axis_size("dp")
    pairs = []
    for i in range(length):
        for tower, sign in ((0, 1), (1, -1)):
            if cores is None or (i % 2) ^ tower == cores:
                pairs.append((2 * i + tower, 2 * ((i + sign * step) % length) + tower))
    return lax.ppermute(array, ("dp", "tower"), pairs)


def swapped(name, array):
    with jax.named_scope(name):
        return lax.ppermute(array, "tower", [(0, 1), (1, 0)])


def onward(name, array):
    with jax.named_scope(name):
        return moved(array, 1)


def back(name, array):
    with jax.named_scope(name):
        return moved(array, -1)


def chip_onward(name, array):
    with jax.named_scope(name):
        return moved(array, 2, 0)


def core_onward(name, array):
    with jax.named_scope(name):
        return moved(array, 1, 0)


def after(array, token):
    return lax.optimization_barrier((array, token))[0]


def inverse_norm_of(rows):
    return lax.rsqrt(jnp.sum(rows * rows, axis=-1, keepdims=True) + epsilon)


def normed_rows(rows):
    rows = rows.astype(jnp.float32)
    return (rows * inverse_norm_of(rows)).astype(jnp.bfloat16)


def norm_kernel(parts, place_ref, lead_ref, features_ref, out_ref, *part_refs):
    tower, core = place_ref[0], place_ref[1]
    for tile in range(2 * PER_BLOCK):
        block, within = tile // PER_BLOCK, tile % PER_BLOCK
        start = pl.multiple_of((block ^ tower) * ROWS + within * TILE, TILE)
        out_ref[pl.ds(tile * TILE, TILE), :] = normed_rows(features_ref[0, pl.ds(start, TILE), :])
    for (second, start, size), part_ref in zip(parts, part_refs):
        block = (core if second else 1 - core) ^ tower
        part_ref[...] = out_ref[pl.ds(pl.multiple_of(block * ROWS + start, LANES), size), :]


def norm_rows(place, lead, features, parts):
    width = features.shape[-1]
    sizes = [2 * ROWS] + [n for _, _, n in parts]
    return pl.pallas_call(
        functools.partial(norm_kernel, parts),
        out_shape=[jax.ShapeDtypeStruct((n, width), jnp.bfloat16) for n in sizes],
        in_specs=[SMEM, ANY, VMEM],
        out_specs=[VMEM] * len(sizes),
        compiler_params=pltpu.CompilerParams(vmem_limit_bytes=VMEM_LIMIT),
    )(place, lead, features)


def label_kernel(blocks_ref, labels_ref, own_ref, other_ref):
    per_block = ROWS // LANES
    for slot in range(8):
        for i in range(per_block):
            line = labels_ref[pl.ds(blocks_ref[slot] * per_block + i, 1), :]
            if slot < 6:
                other_ref[slot, :, pl.ds(i * LANES, LANES)] = line
            else:
                rows = pl.ds((slot - 6) * ROWS + i * LANES, LANES)
                own_ref[rows, :] = jnp.transpose(jnp.broadcast_to(line, (LANES, LANES)))


def label_rows(blocks, labels):
    return pl.pallas_call(
        label_kernel,
        out_shape=[
            jax.ShapeDtypeStruct((2 * ROWS, LANES), jnp.int32),
            jax.ShapeDtypeStruct((6, 1, ROWS), jnp.int32),
        ],
        in_specs=[SMEM, VMEM],
        out_specs=[VMEM, VMEM],
        compiler_params=pltpu.CompilerParams(vmem_limit_bytes=VMEM_LIMIT),
    )(blocks, labels.reshape(-1, LANES))


def update_kernel(pieces, spans, raw, has_old, finish, place_ref, sharpness_ref, shift_ref, *refs):
    refs = list(refs)
    own_ref, own_label_ref, other_label_ref = refs[:3]
    del refs[:3]
    tower, role = place_ref[0], place_ref[2]
    sharpness, shift = sharpness_ref[0], shift_ref[0]
    chunk_refs = [[refs.pop(0) for _ in range(count)] for _, _, _, count in pieces]
    old_ref = refs.pop(0) if has_old else None
    if finish:
        features_ref, out_ref, others_ref, staging, sems = refs
    else:
        out_ref, others_ref = refs
    at, labels = 0, []
    for (slot, start, size, _), choices in zip(pieces, chunk_refs):
        rows = pl.ds(at, size)
        if len(choices) == 1:
            others_ref[rows, :] = choices[0][...]
        else:

            @pl.when(role == 0)
            def _():
                others_ref[rows, :] = choices[0][...]

            @pl.when(role != 0)
            def _():
                others_ref[rows, :] = choices[1][...]

        if raw:
            others_ref[rows, :] = normed_rows(others_ref[rows, :])
        labels.append(other_label_ref[slot][:, start : start + size])
        at += size
    labels = jnp.concatenate(labels, axis=1)
    copies = []
    tiles = 2 * ROWS // TILE

    def others_of(tile):
        low, high = spans[tile // PER_BLOCK]
        return others_ref[pl.ds(low, high - low), :]

    def inner_of(tile):
        own = own_ref[pl.ds(tile * TILE, TILE), :]
        return lax.dot_general(
            own, others_of(tile), (((1,), (1,)), ((), ())), preferred_element_type=jnp.float32
        )

    upcoming = inner_of(0)
    for tile in range(tiles):
        block, within = tile // PER_BLOCK, tile % PER_BLOCK
        low, high = spans[block]
        rows = pl.ds(tile * TILE, TILE)
        inner = upcoming
        if tile + 1 < tiles:
            upcoming = inner_of(tile + 1)
        logit = inner * sharpness + shift
        same = own_label_ref[rows, :1] == labels[:, low:high]
        grown = jnp.exp(jnp.where(same, logit, -logit))
        weight = (jnp.where(same, -sharpness, sharpness) / (1.0 + grown)).astype(jnp.bfloat16)
        total = jnp.dot(weight, others_of(tile), preferred_element_type=jnp.float32)
        if has_old:
            total = old_ref[rows, :] + total
        if not finish:
            out_ref[rows, :] = total
            continue
        native = pl.ds(pl.multiple_of((block ^ tower) * ROWS + within * TILE, TILE), TILE)
        raw = features_ref[0, native, :].astype(jnp.float32)
        inverse_norm = inverse_norm_of(raw)
        unit = raw * inverse_norm
        projected = jnp.sum(unit * total, axis=-1, keepdims=True)
        staging[tile] = inverse_norm * (total - unit * projected)
        copy = pltpu.make_async_copy(staging.at[tile], out_ref.at[0, native, :], sems.at[tile])
        copy.start()
        copies.append(copy)
    for copy in copies:
        copy.wait()


def update(scalars, own, own_labels, other_labels, pieces, spans, grads, raw=False, features=None):
    width = own.shape[-1]
    finish = features is not None
    chunks = [array for *_, arrays in pieces for array in arrays]
    pieces = [(slot, start, size, len(arrays)) for slot, start, size, arrays in pieces]
    operands = [*scalars, own, own_labels, other_labels, *chunks]
    if grads is not None:
        operands.append(grads)
    depth = sum(size for _, _, size, _ in pieces)
    scratch = [pltpu.VMEM((depth, width), jnp.bfloat16)]
    if finish:
        operands.append(features)
        tiles = 2 * ROWS // TILE
        scratch += [pltpu.VMEM((tiles, TILE, width), jnp.float32), pltpu.SemaphoreType.DMA((tiles,))]
    shape = (1, 2 * ROWS, width) if finish else (2 * ROWS, width)
    return pl.pallas_call(
        functools.partial(update_kernel, pieces, spans, raw, grads is not None, finish),
        out_shape=jax.ShapeDtypeStruct(shape, jnp.float32),
        in_specs=[SMEM] * len(scalars) + [VMEM] * (len(operands) - len(scalars)),
        out_specs=ANY if finish else VMEM,
        scratch_shapes=scratch,
        compiler_params=pltpu.CompilerParams(vmem_limit_bytes=VMEM_LIMIT),
        cost_estimate=pl.CostEstimate(flops=1, bytes_accessed=1, transcendentals=0),
    )(*operands)


def per_device(feature_vectors, sample_source_label, sharpness_factor_array, logit_offset_array):
    tower = lax.axis_index("tower")
    dp = lax.axis_index("dp")
    core = dp % 2
    role = core ^ tower
    place = jnp.stack([tower, core, role]).astype(jnp.int32)

    a0, a1 = (n for _, n in FIRST)
    b0, b1 = (n for _, n in SECOND)
    lead = lax.dynamic_slice_in_dim(feature_vectors[0], (1 - core) * ROWS, a0)
    parts = [(False, *FIRST[1]), (True, *SECOND[0]), (True, *SECOND[1])]
    normed, part, *early = norm_rows(place, lead, feature_vectors, parts)

    def block_at(index):
        chip = 4 * (dp // 2)
        return jnp.where(tower == 0, chip + index, chip + 3 - index) % N_BLOCKS

    held = [1 + role, 3 * role - 2, 5 * role - 3, role - 1, 3 * role, -role, 2 * role, 2 * role + 1]
    blocks = jnp.stack([block_at(index) for index in held]).astype(jnp.int32)
    own_labels, other_labels = label_rows(blocks, sample_source_label)
    scalars = (place, sharpness_factor_array, logit_offset_array)
    run = functools.partial(update, scalars, normed, own_labels, other_labels)

    y0 = swapped("y0", lead)
    y1 = swapped("y1", part)
    y0 = after(y0, normed)
    e0, e1 = back("e0", early[0]), back("e1", after(early[1], y0))
    y2 = swapped("y2", e0)
    x0, w0 = onward("x0", y0), chip_onward("w0", y0)

    cut0, cut1 = FIRST
    cut2, cut3 = SECOND
    grads = run(
        [(A, *cut0, (w0, y0)), (X, *cut0, (x0,)), (Y1, *cut0, (y0,))], ((0, 2 * a0), (a0, 3 * a0)), None, raw=True
    )
    y1 = after(y1, x0)
    x1, w1 = onward("x1", y1), chip_onward("w1", y1)
    y2 = after(y2, grads)
    y3 = swapped("y3", after(e1, grads))
    z2, c2 = back("z2", y2), core_onward("c2", y2)
    pieces = [(X, *cut1, (x1,)), (Y2, *cut2, (y2,)), (Y1, *cut1, (y1,))]
    grads = run(pieces, ((0, a1 + b0), (0, 2 * a1 + b0)), grads)
    y3 = after(y3, grads)
    z3, c3 = back("z3", y3), core_onward("c3", y3)
    pieces = [(A, *cut1, (w1, y1)), (B, *cut2, (z2, c2)), (Y2, *cut3, (y3,)), (Z, *cut2, (z2,))]
    grads = run(pieces, ((0, a1 + b0 + b1), (a1 + b0, a1 + 2 * b0 + b1)), grads)
    pieces = [(B, *cut3, (z3, c3)), (Z, *cut3, (z3,))]
    return run(pieces, ((0, b1), (b1, 2 * b1)), grads, features=feature_vectors)


def solution(mesh):
    placed = (P("tower", ("replica", "dp"), None), P("replica"), P(), P())
    return jax.shard_map(
        per_device,
        mesh=mesh,
        in_specs=placed,
        out_specs=P("tower", ("replica", "dp"), None),
        check_vma=False,
    )
```

```python
import functools

import jax
import jax.numpy as jnp
from jax import lax
from jax.experimental import pallas as pl
from jax.experimental.pallas import tpu as pltpu
from jax.sharding import PartitionSpec as P

ROWS = 640
N_BLOCKS = 128
LANES = 128
TILE = 320
PER_BLOCK = ROWS // TILE
VMEM_LIMIT = 16 * 2**20
epsilon = 1e-06

FIRST = ((0, 256), (256, 384))
SECOND = ((0, 384), (384, 256))

VMEM = pl.BlockSpec(memory_space=pltpu.VMEM)
SMEM = pl.BlockSpec(memory_space=pltpu.SMEM)
ANY = pl.BlockSpec(memory_space=pl.ANY)

Y1, X, A, Y2, Z, B = range(6)


def moved(array, step, cores=None):
    length = lax.axis_size("dp")
    pairs = []
    for i in range(length):
        for tower, sign in ((0, 1), (1, -1)):
            if cores is None or (i % 2) ^ tower == cores:
                pairs.append((2 * i + tower, 2 * ((i + sign * step) % length) + tower))
    return lax.ppermute(array, ("dp", "tower"), pairs)


def swapped(name, array):
    with jax.named_scope(name):
        return lax.ppermute(array, "tower", [(0, 1), (1, 0)])


def onward(name, array):
    with jax.named_scope(name):
        return moved(array, 1)


def back(name, array):
    with jax.named_scope(name):
        return moved(array, -1)


def chip_onward(name, array):
    with jax.named_scope(name):
        return moved(array, 2, 0)


def core_onward(name, array):
    with jax.named_scope(name):
        return moved(array, 1, 0)


def after(array, token):
    return lax.optimization_barrier((array, token))[0]


def inverse_norm_of(rows):
    return lax.rsqrt(jnp.sum(rows * rows, axis=-1, keepdims=True) + epsilon)


def normed_rows(rows):
    rows = rows.astype(jnp.float32)
    return (rows * inverse_norm_of(rows)).astype(jnp.bfloat16)


def lead_kernel(features_ref, out_ref, sem):
    start = pl.multiple_of((1 - lax.axis_index("dp") % 2) * ROWS, ROWS)
    copy = pltpu.make_async_copy(features_ref.at[0, pl.ds(start, out_ref.shape[0]), :], out_ref, sem)
    copy.start()
    copy.wait()


def lead_rows(features, count):
    return pl.pallas_call(
        lead_kernel,
        out_shape=jax.ShapeDtypeStruct((count, features.shape[-1]), features.dtype),
        in_specs=[ANY],
        out_specs=VMEM,
        scratch_shapes=[pltpu.SemaphoreType.DMA],
        compiler_params=pltpu.CompilerParams(vmem_limit_bytes=60 * 2**20),
    )(features)


def norm_kernel(parts, place_ref, lead_ref, features_ref, out_ref, *part_refs):
    tower, core = place_ref[0], place_ref[1]
    for tile in range(2 * PER_BLOCK):
        block, within = tile // PER_BLOCK, tile % PER_BLOCK
        start = pl.multiple_of((block ^ tower) * ROWS + within * TILE, TILE)
        out_ref[pl.ds(tile * TILE, TILE), :] = normed_rows(features_ref[0, pl.ds(start, TILE), :])
    for (second, start, size), part_ref in zip(parts, part_refs):
        block = (core if second else 1 - core) ^ tower
        part_ref[...] = out_ref[pl.ds(pl.multiple_of(block * ROWS + start, LANES), size), :]


def norm_rows(place, lead, features, parts):
    width = features.shape[-1]
    sizes = [2 * ROWS] + [n for _, _, n in parts]
    return pl.pallas_call(
        functools.partial(norm_kernel, parts),
        out_shape=[jax.ShapeDtypeStruct((n, width), jnp.bfloat16) for n in sizes],
        in_specs=[SMEM, ANY, VMEM],
        out_specs=[VMEM] * len(sizes),
        compiler_params=pltpu.CompilerParams(vmem_limit_bytes=VMEM_LIMIT),
    )(place, lead, features)


def label_kernel(blocks_ref, labels_ref, own_ref, other_ref):
    per_block = ROWS // LANES
    for slot in range(8):
        for i in range(per_block):
            line = labels_ref[pl.ds(blocks_ref[slot] * per_block + i, 1), :]
            if slot < 6:
                other_ref[slot, :, pl.ds(i * LANES, LANES)] = line
            else:
                rows = pl.ds((slot - 6) * ROWS + i * LANES, LANES)
                own_ref[rows, :] = jnp.transpose(jnp.broadcast_to(line, (LANES, LANES)))


def label_rows(blocks, labels):
    return pl.pallas_call(
        label_kernel,
        out_shape=[
            jax.ShapeDtypeStruct((2 * ROWS, LANES), jnp.int32),
            jax.ShapeDtypeStruct((6, 1, ROWS), jnp.int32),
        ],
        in_specs=[SMEM, VMEM],
        out_specs=[VMEM, VMEM],
        compiler_params=pltpu.CompilerParams(vmem_limit_bytes=VMEM_LIMIT),
    )(blocks, labels.reshape(-1, LANES))


def update_kernel(pieces, spans, raw, has_old, finish, place_ref, sharpness_ref, shift_ref, *refs):
    refs = list(refs)
    own_ref, own_label_ref, other_label_ref = refs[:3]
    del refs[:3]
    tower, role = place_ref[0], place_ref[2]
    sharpness, shift = sharpness_ref[0], shift_ref[0]
    chunk_refs = [[refs.pop(0) for _ in range(count)] for _, _, _, count in pieces]
    old_ref = refs.pop(0) if has_old else None
    if finish:
        features_ref, out_ref, others_ref, staging, sems = refs
    else:
        out_ref, others_ref = refs
    at, labels = 0, []
    for index, ((slot, start, size, _), choices) in enumerate(zip(pieces, chunk_refs)):
        rows = pl.ds(at, size)
        if len(choices) == 1:
            others_ref[rows, :] = choices[0][...]
        else:

            @pl.when(role == 0)
            def _():
                others_ref[rows, :] = choices[0][...]

            @pl.when(role != 0)
            def _():
                others_ref[rows, :] = choices[1][...]

        if index < raw:
            others_ref[rows, :] = normed_rows(others_ref[rows, :])
        labels.append(other_label_ref[slot][:, start : start + size])
        at += size
    labels = jnp.concatenate(labels, axis=1)
    copies = []
    tiles = 2 * ROWS // TILE

    def others_of(tile):
        low, high = spans[tile // PER_BLOCK]
        return others_ref[pl.ds(low, high - low), :]

    def inner_of(tile):
        own = own_ref[pl.ds(tile * TILE, TILE), :]
        return lax.dot_general(
            own, others_of(tile), (((1,), (1,)), ((), ())), preferred_element_type=jnp.float32
        )

    upcoming = inner_of(0)
    for tile in range(tiles):
        block, within = tile // PER_BLOCK, tile % PER_BLOCK
        low, high = spans[block]
        rows = pl.ds(tile * TILE, TILE)
        inner = upcoming
        if tile + 1 < tiles:
            upcoming = inner_of(tile + 1)
        logit = inner * sharpness + shift
        same = own_label_ref[rows, :1] == labels[:, low:high]
        grown = jnp.exp(jnp.where(same, logit, -logit))
        weight = (jnp.where(same, -sharpness, sharpness) / (1.0 + grown)).astype(jnp.bfloat16)
        total = jnp.dot(weight, others_of(tile), preferred_element_type=jnp.float32)
        if has_old:
            total = old_ref[rows, :] + total
        if not finish:
            out_ref[rows, :] = total
            continue
        native = pl.ds(pl.multiple_of((block ^ tower) * ROWS + within * TILE, TILE), TILE)
        raw = features_ref[0, native, :].astype(jnp.float32)
        inverse_norm = inverse_norm_of(raw)
        unit = raw * inverse_norm
        projected = jnp.sum(unit * total, axis=-1, keepdims=True)
        staging[tile] = inverse_norm * (total - unit * projected)
        copy = pltpu.make_async_copy(staging.at[tile], out_ref.at[0, native, :], sems.at[tile])
        copy.start()
        copies.append(copy)
    for copy in copies:
        copy.wait()


def update(scalars, own, own_labels, other_labels, pieces, spans, grads, raw=0, features=None):
    width = own.shape[-1]
    finish = features is not None
    chunks = [array for *_, arrays in pieces for array in arrays]
    pieces = [(slot, start, size, len(arrays)) for slot, start, size, arrays in pieces]
    operands = [*scalars, own, own_labels, other_labels, *chunks]
    if grads is not None:
        operands.append(grads)
    depth = sum(size for _, _, size, _ in pieces)
    scratch = [pltpu.VMEM((depth, width), jnp.bfloat16)]
    if finish:
        operands.append(features)
        tiles = 2 * ROWS // TILE
        scratch += [pltpu.VMEM((tiles, TILE, width), jnp.float32), pltpu.SemaphoreType.DMA((tiles,))]
    shape = (1, 2 * ROWS, width) if finish else (2 * ROWS, width)
    return pl.pallas_call(
        functools.partial(update_kernel, pieces, spans, raw, grads is not None, finish),
        out_shape=jax.ShapeDtypeStruct(shape, jnp.float32),
        in_specs=[SMEM] * len(scalars) + [VMEM] * (len(operands) - len(scalars)),
        out_specs=ANY if finish else VMEM,
        scratch_shapes=scratch,
        compiler_params=pltpu.CompilerParams(vmem_limit_bytes=VMEM_LIMIT),
        cost_estimate=pl.CostEstimate(flops=1, bytes_accessed=1, transcendentals=0),
    )(*operands)


def per_device(feature_vectors, sample_source_label, sharpness_factor_array, logit_offset_array):
    tower = lax.axis_index("tower")
    dp = lax.axis_index("dp")
    core = dp % 2
    role = core ^ tower
    place = jnp.stack([tower, core, role]).astype(jnp.int32)

    a0, a1 = (n for _, n in FIRST)
    b0, b1 = (n for _, n in SECOND)
    lead = lead_rows(feature_vectors, a0)
    parts = [(False, *FIRST[1]), (True, *SECOND[0]), (True, *SECOND[1])]
    normed, part, *early = norm_rows(place, lead, feature_vectors, parts)

    def block_at(index):
        chip = 4 * (dp // 2)
        return jnp.where(tower == 0, chip + index, chip + 3 - index) % N_BLOCKS

    held = [1 + role, 3 * role - 2, 5 * role - 3, role - 1, 3 * role, -role, 2 * role, 2 * role + 1]
    blocks = jnp.stack([block_at(index) for index in held]).astype(jnp.int32)
    own_labels, other_labels = label_rows(blocks, sample_source_label)
    scalars = (place, sharpness_factor_array, logit_offset_array)
    run = functools.partial(update, scalars, normed, own_labels, other_labels)

    y0 = swapped("y0", lead)
    y1 = swapped("y1", part)
    y0 = after(y0, (normed, own_labels, other_labels))
    e0, e1 = back("e0", early[0]), back("e1", after(early[1], y0))
    y2 = swapped("y2", e0)
    x0, w0 = onward("x0", y0), chip_onward("w0", y0)

    cut0, cut1 = FIRST
    cut2, cut3 = SECOND
    y1 = after(y1, x0)
    x1, w1 = onward("x1", y1), chip_onward("w1", y1)
    pieces = [(A, *cut0, (w0, y0)), (X, *cut0, (x0,)), (Y1, *cut0, (y0,)), (Y1, *cut1, (y1,))]
    grads = run(pieces, ((0, 2 * a0), (a0, 3 * a0 + a1)), None, raw=3)
    y2 = after(y2, grads)
    y3 = swapped("y3", e1)
    z2, c2 = back("z2", y2), core_onward("c2", y2)
    grads = run([(X, *cut1, (x1,)), (Y2, *cut2, (y2,))], ((0, a1 + b0), (0, a1 + b0)), grads)
    y3 = after(y3, grads)
    z3, c3 = back("z3", y3), core_onward("c3", y3)
    pieces = [(A, *cut1, (w1, y1)), (B, *cut2, (z2, c2)), (Y2, *cut3, (y3,)), (Z, *cut2, (z2,))]
    grads = run(pieces, ((0, a1 + b0 + b1), (a1 + b0, a1 + 2 * b0 + b1)), grads)
    z3 = after(z3, grads)
    pieces = [(B, *cut3, (z3, c3)), (Z, *cut3, (z3,))]
    return run(pieces, ((0, b1), (b1, 2 * b1)), grads, features=feature_vectors)


def solution(mesh):
    placed = (P("tower", ("replica", "dp"), None), P("replica"), P(), P())
    return jax.shard_map(
        per_device,
        mesh=mesh,
        in_specs=placed,
        out_specs=P("tower", ("replica", "dp"), None),
        check_vma=False,
    )
```
